256 devices in a mesh: section: 8 (over z), rows: 32 (over y, x, core).
Axes of the slice: x: 4, y: 4, z: 8, core: 2. Of those that a mesh axis runs over, the one named last changes fastest.
Arguments:
- latents: bfloat16 [8, 2, 32, 48, 384], P('section', None, 'rows'), may hold values from -6 to 6
- conv_weight: bfloat16 [8, 3, 3, 3, 384, 384], P('section'), may hold values from -0.0625 to 0.0625
- gain: float32 [8, 384], P('section'), may hold values from 0.5 to 2
- bias: float32 [8, 384], P('section'), may hold values from -0.5 to 0.5
Outputs:
- decoded: bfloat16 [8, 2, 32, 48, 384], P('section', None, 'rows')
The draws below stay inside these ranges and needn't reach their ends.
All inputs are finite; a program needn't handle non-finite values.
Results may differ from the reference program's by a relative error of at most 0.017.
Values may be sent and summed in bfloat16 or wider, within the bound.
No kernel may reach another device: no remote copies, remote signals or barrier semaphores. Data moves between devices by JAX's collectives and lax.ppermute only.
A program may use at most 64 MiB of HBM per device.

```python
import math
import jax
import jax.numpy as jnp
from jax import lax

C = 384
F = 2
W = 48
SECTIONS = 8
BLOCKS = 8
H = 32


def block_scale(key, extent, cuts, low, largest):
    def one(axis_at, blocks):
        heights = jax.random.uniform(jax.random.fold_in(jax.random.fold_in(key, 6), axis_at), (blocks,), jnp.float32, low / len(cuts), largest / len(cuts))
        return jnp.repeat(jnp.exp(heights), extent[axis_at] // blocks).reshape((-1,) + (1,) * (len(extent) - axis_at - 1))

    level = one(*cuts[0])
    for cut in cuts[1:]:
        level = level * one(*cut)
    return level


def noise(key, shape, scale, reach, shards=(), dtype=jnp.bfloat16):
    level = block_scale(key, shape, shards, -0.22, 0.18) if shards else 1.0
    values = jax.random.normal(key, shape, jnp.float32) * scale * level
    return jnp.minimum(jnp.maximum(values, -reach), reach).astype(dtype)


def setup_inputs(seed: int = 0) -> dict:
    streams_of = jax.random.split(jax.random.key(seed), 5)
    latents = noise(streams_of[0], (BLOCKS, F, H, W, C), 1.0, 6.0, ((0, 8), (2, 32)))
    conv_weight = noise(streams_of[1], (SECTIONS, 3, 3, 3, C, C), (27 * C) ** -0.5, 0.0625, ((0, 8),))
    gain = jnp.clip(jnp.exp(math.log(2.0) - 1.3862944 * jax.random.uniform(streams_of[2], (SECTIONS, C), jnp.float32) ** block_scale(streams_of[2], (SECTIONS, C), ((0, 8),), -0.2, 0.2)), 0.5, 2.0)
    bias = jnp.clip(jax.random.uniform(streams_of[3], (SECTIONS, C), jnp.float32, -0.5, 0.5) * block_scale(streams_of[3], (SECTIONS, C), ((0, 8),), -0.4, 0.0), -0.5, 0.5)
    return {"latents": latents, "conv_weight": conv_weight, "gain": gain, "bias": bias}


epsilon = 1e-06

def normed_silu(values, gain_row):
    widened = values.astype(jnp.float32)
    mean_square = lax.optimization_barrier(jnp.mean(widened * widened, axis=-1, keepdims=True))
    return jax.nn.silu(widened * lax.rsqrt(mean_square + epsilon) * gain_row).astype(jnp.bfloat16)

def reference(latents, conv_weight, gain, bias):
    blocks, frames, height, columns, channels = latents.shape
    all_frames = blocks * frames
    current = latents.reshape(all_frames, height, columns, channels)
    for section_idx in range(conv_weight.shape[0]):
        activated = normed_silu(current, gain[section_idx])
        padded = jnp.pad(activated, ((2, 0), (1, 1), (1, 1), (0, 0)))
        total = jnp.zeros((all_frames * height * columns, channels), jnp.float32)
        for tap_t in range(3):
            for tap_r in range(3):
                for tap_c in range(3):
                    piece = padded[tap_t:tap_t + all_frames, tap_r:tap_r + height, tap_c:tap_c + columns]
                    total = total + jnp.dot(piece.reshape(-1, channels), conv_weight[section_idx, tap_t, tap_r, tap_c], preferred_element_type=jnp.float32)
        summed = current.astype(jnp.float32) + total.reshape(all_frames, height, columns, channels) + bias[section_idx]
        current = summed.astype(jnp.bfloat16)
    return current.reshape(latents.shape)
```

```python
import functools
import jax
import jax.numpy as jnp
from jax import lax
from jax.experimental import pallas as pl
from jax.experimental.pallas import tpu as pltpu
from jax.sharding import PartitionSpec as P

epsilon = 1e-06
GROUP = 2
CORES = 2
CHIPS_X = 4
OWN, OTHER, HALO = range(3)
STEP, SECTION, ODD, EDGE = range(4)
mebi = 1024 * 1024
whole = pl.BlockSpec(memory_space=pltpu.VMEM)


def activated(widened, gain_row):
    mean_square = jnp.mean(widened * widened, axis=-1, keepdims=True)
    normed = widened * lax.rsqrt(mean_square + epsilon) * gain_row
    return normed / (1.0 + jnp.exp(-normed))


def fill(taps, place, values, past, gain, keep):
    rows, chans = values.shape
    cols = past.shape[0] // 2
    kept = 2 * cols
    starts = place[STEP : STEP + 1, :1] == place[SECTION : SECTION + 1, :1]
    old = past[...].astype(jnp.float32)
    taps[:kept] = jnp.where(starts, 0.0, old).astype(jnp.bfloat16)
    act = activated(values, gain[...])
    if keep is not None:
        act = jnp.where(keep, act, 0.0)
    col = lax.broadcasted_iota(jnp.int32, (rows, chans), 0) % cols
    left = jnp.where(col == 0, 0.0, pltpu.roll(act, 1, 0))
    right = jnp.where(col == cols - 1, 0.0, pltpu.roll(act, rows - 1, 0))
    taps[kept:, :chans] = left.astype(jnp.bfloat16)
    taps[kept:, chans : 2 * chans] = act.astype(jnp.bfloat16)
    taps[kept:, 2 * chans :] = right.astype(jnp.bfloat16)


def add_taps(total, taps, weight, tap_r, cols):
    for i in range(3):
        total += jnp.dot(
            taps[i * cols : i * cols + total.shape[0], :],
            weight[3 * i + tap_r],
            preferred_element_type=jnp.float32,
        )
    return total


def current(which, place, pending, arrived):
    frames, cols, chans = pending.shape[1:]
    values = pending[which].reshape(frames * cols, chans).astype(jnp.float32)
    if arrived is not None:
        came = arrived[...].reshape(frames * cols, chans).astype(jnp.float32)
        values = jnp.where(place[SECTION : SECTION + 1, :1] == 0, values, came)
    return values


def near_kernel(fresh, place, pending, weight, gain, bias, past_own, past_halo, *rest):
    own, halo = (None, None) if fresh else rest[:2]
    total_out, recent_own, recent_halo, taps_own, taps_halo = rest[-5:]
    cols = pending.shape[2]
    values = current(OWN, place, pending, own)
    rows = values.shape[0]
    fill(taps_own, place, values, past_own, gain, None)
    edge = current(HALO, place, pending, halo)
    fill(taps_halo, place, edge, past_halo, gain, place[EDGE : EDGE + 1, :1] == 0)
    total = add_taps(values + bias[...], taps_own, weight, 1, cols)
    total_out[...] = add_taps(total, taps_halo, weight, 2 * place[ODD, 0], cols)
    recent_own[...] = taps_own[rows:, :]
    recent_halo[...] = taps_halo[rows:, :]


def last_kernel(fresh, place, pending, weight, gain, total, past, *rest):
    other = None if fresh else rest[0]
    sent, recent, next_place, taps = rest[-4:]
    frames, cols, chans = sent.shape
    fill(taps, place, current(OTHER, place, pending, other), past, gain, None)
    result = add_taps(total[...], taps, weight, 2 - 2 * place[ODD, 0], cols)
    sent[...] = result.astype(jnp.bfloat16).reshape(frames, cols, chans)
    recent[...] = taps[frames * cols :, :]
    line = lax.broadcasted_iota(jnp.int32, place.shape, 0)
    next_place[...] = place[...] + jnp.where(line == STEP, 1, 0)


def call(kernel, name, operands, out_shape, taps):
    return pl.pallas_call(
        kernel,
        out_shape=out_shape,
        in_specs=[whole] * len(operands),
        out_specs=[whole] * len(out_shape),
        scratch_shapes=[pltpu.VMEM(taps[1:], jnp.bfloat16)] * taps[0],
        compiler_params=pltpu.CompilerParams(vmem_limit_bytes=16 * mebi),
        cost_estimate=pl.CostEstimate(flops=0, bytes_accessed=0, transcendentals=0),
        name=name,
    )(*operands)


def near_rows(place, pending, weight, gain, bias, past_own, past_halo, own, halo):
    frames, cols, chans = pending.shape[1:]
    operands = [place, pending, weight, gain, bias, past_own, past_halo]
    fresh = own is None
    if not fresh:
        operands += [own, halo]
    recent = jax.ShapeDtypeStruct(past_own.shape, jnp.bfloat16)
    out_shape = [jax.ShapeDtypeStruct((frames * cols, chans), jnp.float32), recent, recent]
    kernel = functools.partial(near_kernel, fresh)
    return call(kernel, "near_rows", operands, out_shape, (2, (2 + frames) * cols, 3 * chans))


def last_row(place, pending, weight, gain, total, past, other):
    frames, cols, chans = pending.shape[1:]
    operands = [place, pending, weight, gain, total, past]
    fresh = other is None
    if not fresh:
        operands.append(other)
    out_shape = [
        jax.ShapeDtypeStruct((frames, cols, chans), jnp.bfloat16),
        jax.ShapeDtypeStruct(past.shape, jnp.bfloat16),
        jax.ShapeDtypeStruct(place.shape, place.dtype),
    ]
    kernel = functools.partial(last_kernel, fresh)
    return call(kernel, "last_row", operands, out_shape, (1, (2 + frames) * cols, 3 * chans))


def held(weight):
    def kernel(source, target):
        @pl.loop(0, weight.shape[0])
        def _(at):
            target[at] = source[at]

    return pl.pallas_call(
        kernel,
        out_shape=pltpu.VMEM(weight.shape, weight.dtype),
        in_specs=[whole],
        out_specs=whole,
        compiler_params=pltpu.CompilerParams(vmem_limit_bytes=24 * mebi),
        cost_estimate=pl.CostEstimate(
            flops=0, bytes_accessed=2 * weight.size * 2, transcendentals=0
        ),
        name="held",
    )(weight)


def body(latents, conv_weight, gain, bias):
    sections = lax.axis_size("section")
    row_count = lax.axis_size("rows")
    section_id = lax.axis_index("section")
    row_id = lax.axis_index("rows")
    block_frames, _, cols, chans = latents.shape[1:]
    weight = conv_weight[0].reshape(9, 3 * chans, chans)
    local = latents[0, :, 0]
    items = sections // GROUP
    steps = sections - 1 + items

    def on_walk(r):
        line, at = divmod(r, CHIPS_X * CORES)
        chip, core = divmod(at, CORES)
        return (line * CHIPS_X + (CHIPS_X - 1 - chip if line % 2 else chip)) * CORES + core

    walk = {r: on_walk(r) for r in range(row_count)}
    same_row = {r: r for r in range(row_count)}
    partner = {r: r ^ 1 for r in range(row_count)}
    across = {walk[r]: walk[(r + 1 if r % 2 else r - 1) % row_count] for r in range(row_count)}

    def move(x, by, next_row):
        pairs = [
            (s * row_count + r, by(s) % sections * row_count + next_row[r])
            for s in range(sections)
            for r in range(row_count)
        ]
        return lax.ppermute(x, ("section", "rows"), pairs)

    stay = lambda s: s
    onward = lambda s: s + 1
    swapped = lambda s: s ^ 1
    homeward = lambda s: s - GROUP

    odd = row_id % 2
    edge = (row_id == walk[0]) | (row_id == walk[row_count - 1])
    lines = jnp.stack([jnp.zeros_like(section_id), section_id, odd, edge.astype(jnp.int32)])
    place = jnp.broadcast_to(jnp.pad(lines, (0, 4))[:, None], (8, 128)).astype(jnp.int32)

    first = move(local, stay, walk)
    second = move(local, swapped, walk)
    item = jnp.concatenate([first, second], axis=0)
    halo = move(item, stay, across)
    other = move(item, stay, partner)
    pending = jnp.stack([item, other, halo])
    weight = held(weight)
    pasts = [jnp.zeros((2 * cols, 3 * chans), jnp.bfloat16)] * 3
    own = halo = other = outbox = None
    for step in range(steps):
        if step:
            own, halo = lax.optimization_barrier((own, halo))
            other = move(own, stay, partner)
        total, pasts[OWN], pasts[HALO] = near_rows(
            place, pending, weight, gain, bias, pasts[OWN], pasts[HALO], own, halo
        )
        sent, pasts[OTHER], place = last_row(
            place, pending, weight, gain, total, pasts[OTHER], other
        )
        if step >= sections - 1:
            outbox = sent if outbox is None else jnp.where(section_id == sections - 1, sent, outbox)
        if step + 1 == steps:
            break
        own = move(sent, onward, same_row)
        halo = move(sent, onward, across)
        if step + 1 < items:
            pending = move(pending, homeward, same_row)
        if step >= sections - 1:
            outbox = move(outbox, homeward, same_row)
    early = move(outbox[:block_frames], swapped, walk)
    late = move(outbox[block_frames:], stay, walk)
    decoded = jnp.where(section_id % GROUP == 0, early, late)
    return decoded[None, :, None]


def solution(mesh):
    in_specs = (
        P("section", None, "rows", None, None),
        P("section", None, None, None, None, None),
        P("section", None),
        P("section", None),
    )
    out_specs = P("section", None, "rows", None, None)
    return jax.shard_map(body, mesh=mesh, in_specs=in_specs, out_specs=out_specs, check_vma=False)
```

```python
import functools
import jax
import jax.numpy as jnp
from jax import lax
from jax.experimental import pallas as pl
from jax.experimental.pallas import tpu as pltpu
from jax.sharding import PartitionSpec as P

epsilon = 1e-06
GROUP = 2
CORES = 2
CHIPS_X = 4
OWN, OTHER, HALO = range(3)
STEP, SECTION, ODD, EDGE = range(4)
mebi = 1024 * 1024
whole = pl.BlockSpec(memory_space=pltpu.VMEM)


def activated(widened, gain_row):
    mean_square = jnp.mean(widened * widened, axis=-1, keepdims=True)
    normed = widened * lax.rsqrt(mean_square + epsilon) * gain_row
    return normed / (1.0 + jnp.exp(-normed))


def row_kernel(which, place, arrived, past, weight, gain, extra, *rest):
    taps = rest[-1]
    frames, cols, chans = arrived.shape
    rows = frames * cols
    kept = 2 * cols
    values = arrived[...].reshape(rows, chans).astype(jnp.float32)
    starts = place[STEP : STEP + 1, :1] == place[SECTION : SECTION + 1, :1]
    old = past[...].astype(jnp.float32)
    taps[:kept] = jnp.where(starts, 0.0, old).astype(jnp.bfloat16)
    act = activated(values, gain[...])
    if which == HALO:
        act = jnp.where(place[EDGE : EDGE + 1, :1] > 0, 0.0, act)
    col = lax.broadcasted_iota(jnp.int32, (rows, chans), 0) % cols
    left = jnp.where(col == 0, 0.0, pltpu.roll(act, 1, 0))
    right = jnp.where(col == cols - 1, 0.0, pltpu.roll(act, rows - 1, 0))
    taps[kept:, :chans] = left.astype(jnp.bfloat16)
    taps[kept:, chans : 2 * chans] = act.astype(jnp.bfloat16)
    taps[kept:, 2 * chans :] = right.astype(jnp.bfloat16)
    if which == OWN:
        total = values + extra[...]
        tap_r = 1
    else:
        total = extra[...]
        odd = place[ODD, 0]
        tap_r = 2 * odd if which == HALO else 2 - 2 * odd
    for i in range(3):
        total += jnp.dot(
            taps[i * cols : i * cols + rows, :],
            weight[3 * i + tap_r],
            preferred_element_type=jnp.float32,
        )
    if which == HALO:
        sent, recent, next_place = rest[:-1]
        sent[...] = total.astype(jnp.bfloat16).reshape(frames, cols, chans)
        line = lax.broadcasted_iota(jnp.int32, place.shape, 0)
        next_place[...] = place[...] + jnp.where(line == STEP, 1, 0)
    else:
        total_out, recent = rest[:-1]
        total_out[...] = total
    recent[...] = taps[rows:, :]


def row_taps(which, place, arrived, past, weight, gain, extra):
    frames, cols, chans = arrived.shape
    rows = frames * cols
    operands = [place, arrived, past, weight, gain, extra]
    out_shape = [
        jax.ShapeDtypeStruct((rows, chans), jnp.float32),
        jax.ShapeDtypeStruct(past.shape, jnp.bfloat16),
    ]
    if which == HALO:
        out_shape[0] = jax.ShapeDtypeStruct(arrived.shape, jnp.bfloat16)
        out_shape.append(jax.ShapeDtypeStruct(place.shape, place.dtype))
    return pl.pallas_call(
        functools.partial(row_kernel, which),
        out_shape=out_shape,
        in_specs=[whole] * len(operands),
        out_specs=[whole] * len(out_shape),
        scratch_shapes=[pltpu.VMEM(((2 + frames) * cols, 3 * chans), jnp.bfloat16)],
        compiler_params=pltpu.CompilerParams(vmem_limit_bytes=8 * mebi),
        cost_estimate=pl.CostEstimate(flops=1000, bytes_accessed=1000, transcendentals=0),
        name=("own_row", "other_row", "halo_row")[which],
    )(*operands)


def held(weight):
    def kernel(source, target):
        @pl.loop(0, weight.shape[0])
        def _(at):
            target[at] = source[at]

    return pl.pallas_call(
        kernel,
        out_shape=pltpu.VMEM(weight.shape, weight.dtype),
        in_specs=[whole],
        out_specs=whole,
        compiler_params=pltpu.CompilerParams(vmem_limit_bytes=8 * mebi),
        cost_estimate=pl.CostEstimate(
            flops=0, bytes_accessed=2 * weight.size * 2, transcendentals=0
        ),
        name="held",
    )(weight)


def body(latents, conv_weight, gain, bias):
    sections = lax.axis_size("section")
    row_count = lax.axis_size("rows")
    section_id = lax.axis_index("section")
    row_id = lax.axis_index("rows")
    block_frames, _, cols, chans = latents.shape[1:]
    weight = conv_weight[0].reshape(9, 3 * chans, chans)
    local = latents[0, :, 0]
    items = sections // GROUP
    steps = sections - 1 + items

    def on_walk(r):
        line, at = divmod(r, CHIPS_X * CORES)
        chip, core = divmod(at, CORES)
        return (line * CHIPS_X + (CHIPS_X - 1 - chip if line % 2 else chip)) * CORES + core

    walk = {r: on_walk(r) for r in range(row_count)}
    same_row = {r: r for r in range(row_count)}
    partner = {r: r ^ 1 for r in range(row_count)}
    across = {walk[r]: walk[(r + 1 if r % 2 else r - 1) % row_count] for r in range(row_count)}

    def move(x, by, next_row):
        pairs = [
            (s * row_count + r, by(s) % sections * row_count + next_row[r])
            for s in range(sections)
            for r in range(row_count)
        ]
        return lax.ppermute(x, ("section", "rows"), pairs)

    stay = lambda s: s
    onward = lambda s: s + 1
    swapped = lambda s: s ^ 1
    homeward = lambda s: s if s % GROUP else s - GROUP
    backward = lambda s: s - GROUP if s % GROUP else s

    odd = row_id % 2
    edge = (row_id == walk[0]) | (row_id == walk[row_count - 1])
    lines = jnp.stack([jnp.zeros_like(section_id), section_id, odd, edge.astype(jnp.int32)])
    place = jnp.broadcast_to(jnp.pad(lines, (0, 4))[:, None], (8, 128)).astype(jnp.int32)

    own = jnp.concatenate([move(local, stay, walk), move(local, swapped, walk)], axis=0)
    pending = own
    weight = held(weight)
    pasts = [jnp.zeros((2 * cols, 3 * chans), jnp.bfloat16)] * 3
    outbox = None
    for step in range(steps):
        other = move(own, stay, partner)
        halo = move(own, stay, across)
        total, pasts[OWN] = row_taps(OWN, place, own, pasts[OWN], weight, gain, bias)
        total, pasts[OTHER] = row_taps(OTHER, place, other, pasts[OTHER], weight, gain, total)
        sent, pasts[HALO], place = row_taps(HALO, place, halo, pasts[HALO], weight, gain, total)
        if step >= sections - 1:
            outbox = sent if outbox is None else jnp.where(section_id == sections - 1, sent, outbox)
        if step + 1 == steps:
            break
        own = move(sent, onward, same_row)
        if step + 1 < items:
            pending = move(pending, homeward, same_row)
            own = jnp.where(section_id == 0, pending, own)
        if step >= sections - 1:
            outbox = move(outbox, backward, same_row)
    early = move(outbox[:block_frames], swapped, walk)
    late = move(outbox[block_frames:], stay, walk)
    decoded = jnp.where(section_id % GROUP == 0, early, late)
    return decoded[None, :, None]


def solution(mesh):
    in_specs = (
        P("section", None, "rows", None, None),
        P("section", None, None, None, None, None),
        P("section", None),
        P("section", None),
    )
    out_specs = P("section", None, "rows", None, None)
    return jax.shard_map(body, mesh=mesh, in_specs=in_specs, out_specs=out_specs, check_vma=False)
```

```python
import functools
import jax
import jax.numpy as jnp
from jax import lax
from jax.experimental import pallas as pl
from jax.experimental.pallas import tpu as pltpu
from jax.sharding import PartitionSpec as P

epsilon = 1e-06
LAG = 2
CORES = 2
CHIPS_X = 4
OWN, OTHER, HALO = range(3)
AGE, ODD, EDGE = range(3)
mebi = 1024 * 1024
whole = pl.BlockSpec(memory_space=pltpu.VMEM)


def activated(widened, gain_row):
    mean_square = jnp.mean(widened * widened, axis=-1, keepdims=True)
    normed = widened * lax.rsqrt(mean_square + epsilon) * gain_row
    return normed / (1.0 + jnp.exp(-normed))


def row_kernel(which, turn, place, arrived, past, weight, gain, extra, *rest):
    taps = rest[-1]
    frames, cols, chans = arrived.shape
    rows = frames * cols
    kept = 2 * cols
    values = arrived[...].reshape(rows, chans).astype(jnp.float32)
    age = place[AGE : AGE + 1, :1]
    old = past[...].astype(jnp.float32)
    taps[:kept] = jnp.where(age == 0, 0.0, old).astype(jnp.bfloat16)
    act = activated(values, gain[...])
    if which == HALO:
        act = jnp.where(place[EDGE : EDGE + 1, :1] > 0, 0.0, act)
    col = lax.broadcasted_iota(jnp.int32, (rows, chans), 0) % cols
    left = jnp.where(col == 0, 0.0, pltpu.roll(act, 1, 0))
    right = jnp.where(col == cols - 1, 0.0, pltpu.roll(act, rows - 1, 0))
    taps[kept:, :chans] = left.astype(jnp.bfloat16)
    taps[kept:, chans : 2 * chans] = act.astype(jnp.bfloat16)
    taps[kept:, 2 * chans :] = right.astype(jnp.bfloat16)
    if which == OWN:
        total = values + extra[...]
        tap_r = 1
    else:
        total = extra[...]
        odd = place[ODD, 0]
        tap_r = 2 * odd if which == HALO else 2 - 2 * odd
    for i in range(3):
        total += jnp.dot(
            taps[i * cols : i * cols + rows, :],
            weight[3 * i + tap_r],
            preferred_element_type=jnp.float32,
        )
    if which == HALO:
        own, sent, recent, next_place = rest[:-1]
        as_it_came = own[...].reshape(rows, chans).astype(jnp.float32)
        waits = (age < turn // LAG - turn) | (age >= turn)
        total = jnp.where(waits, as_it_came, total)
        sent[...] = total.astype(jnp.bfloat16).reshape(frames, cols, chans)
        line = lax.broadcasted_iota(jnp.int32, place.shape, 0)
        next_place[...] = place[...] + jnp.where(line == AGE, 1, 0)
    else:
        total_out, recent = rest[:-1]
        total_out[...] = total
    recent[...] = taps[rows:, :]


def row_taps(which, place, arrived, past, weight, gain, *extra):
    frames, cols, chans = arrived.shape
    rows = frames * cols
    operands = [place, arrived, past, weight, gain, *extra]
    turn = LAG * lax.axis_size("section")
    out_shape = [
        jax.ShapeDtypeStruct((rows, chans), jnp.float32),
        jax.ShapeDtypeStruct(past.shape, jnp.bfloat16),
    ]
    if which == HALO:
        out_shape[0] = jax.ShapeDtypeStruct(arrived.shape, jnp.bfloat16)
        out_shape.append(jax.ShapeDtypeStruct(place.shape, place.dtype))
    return pl.pallas_call(
        functools.partial(row_kernel, which, turn),
        out_shape=out_shape,
        in_specs=[whole] * len(operands),
        out_specs=[whole] * len(out_shape),
        scratch_shapes=[pltpu.VMEM(((2 + frames) * cols, 3 * chans), jnp.bfloat16)],
        compiler_params=pltpu.CompilerParams(vmem_limit_bytes=8 * mebi),
        cost_estimate=pl.CostEstimate(flops=1000, bytes_accessed=1000, transcendentals=0),
        name=("own_row", "other_row", "halo_row")[which],
    )(*operands)


def held(weight):
    def kernel(source, target):
        @pl.loop(0, weight.shape[0])
        def _(at):
            target[at] = source[at]

    return pl.pallas_call(
        kernel,
        out_shape=pltpu.VMEM(weight.shape, weight.dtype),
        in_specs=[whole],
        out_specs=whole,
        compiler_params=pltpu.CompilerParams(vmem_limit_bytes=8 * mebi),
        cost_estimate=pl.CostEstimate(
            flops=0, bytes_accessed=2 * weight.size * 2, transcendentals=0
        ),
        name="held",
    )(weight)


def body(latents, conv_weight, gain, bias):
    sections = lax.axis_size("section")
    row_count = lax.axis_size("rows")
    section_id = lax.axis_index("section")
    row_id = lax.axis_index("rows")
    cols, chans = latents.shape[3:]
    weight = conv_weight[0].reshape(9, 3 * chans, chans)
    local = latents[0, :, 0]
    items = sections
    steps = LAG * (sections - 1) + items

    def on_walk(r):
        line, at = divmod(r, CHIPS_X * CORES)
        chip, core = divmod(at, CORES)
        return (line * CHIPS_X + (CHIPS_X - 1 - chip if line % 2 else chip)) * CORES + core

    walk = {r: on_walk(r) for r in range(row_count)}
    same_row = {r: r for r in range(row_count)}
    partner = {r: r ^ 1 for r in range(row_count)}
    across = {walk[r]: walk[(r + 1 if r % 2 else r - 1) % row_count] for r in range(row_count)}
    same_section = {s: s for s in range(sections)}
    onward = {s: (s + 1) % sections for s in range(sections)}

    def move(x, next_section, next_row):
        pairs = [
            (s * row_count + r, next_section[s] * row_count + next_row[r])
            for s in range(sections)
            for r in range(row_count)
        ]
        return lax.ppermute(x, ("section", "rows"), pairs)

    def filled(route):
        route = dict(route)
        targets = set(range(sections)) - set(route.values())
        for s in range(sections):
            if s not in route and s in targets:
                route[s] = s
                targets.remove(s)
        for s in range(sections):
            if s not in route:
                route[s] = targets.pop()
        return route

    def place_of(item, step):
        return (step - item) // LAG % sections

    def entry(step):
        return filled({i: place_of(i, step) for i in range(items) if (step - i) % LAG == 0})

    def exit(step):
        there = [i for i in range(items) if (step - i) % LAG == 0]
        return filled({place_of(i, step): i for i in there}), there

    odd = row_id % 2
    edge = (row_id == walk[0]) | (row_id == walk[row_count - 1])
    lines = jnp.stack([-LAG * section_id, odd, edge.astype(jnp.int32)])
    place = jnp.broadcast_to(jnp.pad(lines, (0, 5))[:, None], (8, 128)).astype(jnp.int32)

    own = {step: move(local, entry(step), walk) for step in range(LAG)}
    weight = held(weight)
    pasts = [jnp.zeros((2 * cols, 3 * chans), jnp.bfloat16)] * 3
    decoded = None
    for step in range(steps):
        mine = own.pop(step)
        other = move(mine, same_section, partner)
        halo = move(mine, same_section, across)
        total, pasts[OWN] = row_taps(OWN, place, mine, pasts[OWN], weight, gain, bias)
        total, pasts[OTHER] = row_taps(OTHER, place, other, pasts[OTHER], weight, gain, total)
        sent, pasts[HALO], place = row_taps(
            HALO, place, halo, pasts[HALO], weight, gain, total, mine
        )
        if step + LAG < steps:
            own[step + LAG] = move(sent, onward, same_row)
        if step >= steps - LAG - 1:
            route, there = exit(step)
            if step == steps - 1:
                route, there = same_section, [items - 1]
            elif step == steps - LAG - 1:
                there = [i for i in there if i != items - 1]
            home = move(sent, route, walk)
            here = functools.reduce(jnp.logical_or, [section_id == i for i in there])
            decoded = home if decoded is None else jnp.where(here, home, decoded)
    return decoded[None, :, None]


def solution(mesh):
    in_specs = (
        P("section", None, "rows", None, None),
        P("section", None, None, None, None, None),
        P("section", None),
        P("section", None),
    )
    out_specs = P("section", None, "rows", None, None)
    return jax.shard_map(body, mesh=mesh, in_specs=in_specs, out_specs=out_specs, check_vma=False)
```

```python
import functools
import jax
import jax.numpy as jnp
from jax import lax
from jax.experimental import pallas as pl
from jax.experimental.pallas import tpu as pltpu
from jax.sharding import PartitionSpec as P

epsilon = 1e-06
LAG = 2
CORES = 2
CHIPS_X = 4
OWN, OTHER, HALO = range(3)
AGE, ODD, EDGE = range(3)
mebi = 1024 * 1024
whole = pl.BlockSpec(memory_space=pltpu.VMEM)


def activated(widened, gain_row):
    mean_square = jnp.mean(widened * widened, axis=-1, keepdims=True)
    normed = widened * lax.rsqrt(mean_square + epsilon) * gain_row
    return normed / (1.0 + jnp.exp(-normed))


def layer_kernel(turn, last, place, own, other, halo, past, weight, gain, bias, handed, *rest):
    sent, taps = rest[0], rest[-1]
    frames, cols, chans = own.shape
    rows = frames * cols
    kept = 2 * cols
    age = place[AGE : AGE + 1, :1]
    col = lax.broadcasted_iota(jnp.int32, (rows, chans), 0) % cols
    values = own[...].reshape(rows, chans).astype(jnp.float32)
    total = values + bias[...]
    odd = place[ODD, 0]
    for which, arrived in enumerate((own, other, halo)):
        if which != OWN:
            values = arrived[...].reshape(rows, chans).astype(jnp.float32)
        old = past[which].astype(jnp.float32)
        taps[which, :kept] = jnp.where(age == 0, 0.0, old).astype(jnp.bfloat16)
        act = activated(values, gain[...])
        if which == HALO:
            act = jnp.where(place[EDGE : EDGE + 1, :1] > 0, 0.0, act)
        left = jnp.where(col == 0, 0.0, pltpu.roll(act, 1, 0))
        right = jnp.where(col == cols - 1, 0.0, pltpu.roll(act, rows - 1, 0))
        taps[which, kept:, :chans] = left.astype(jnp.bfloat16)
        taps[which, kept:, chans : 2 * chans] = act.astype(jnp.bfloat16)
        taps[which, kept:, 2 * chans :] = right.astype(jnp.bfloat16)
        tap_r = (1, 2 - 2 * odd, 2 * odd)[which]
        for i in range(3):
            total += jnp.dot(
                taps[which, i * cols : i * cols + rows, :],
                weight[3 * i + tap_r],
                preferred_element_type=jnp.float32,
            )
    as_it_came = handed[...].reshape(rows, chans).astype(jnp.float32)
    waits = (age < turn // LAG - turn) | (age >= turn)
    total = jnp.where(waits, as_it_came, total)
    sent[...] = total.astype(jnp.bfloat16).reshape(frames, cols, chans)
    if not last:
        recent, next_place = rest[1:3]
        recent[...] = taps[:, rows:, :]
        line = lax.broadcasted_iota(jnp.int32, place.shape, 0)
        next_place[...] = place[...] + jnp.where(line == AGE, 1, 0)


def layer(last, place, own, other, halo, past, weight, gain, bias, handed):
    frames, cols, chans = own.shape
    turn = LAG * lax.axis_size("section")
    operands = [place, own, other, halo, past, weight, gain, bias, handed]
    out_shape = [jax.ShapeDtypeStruct(own.shape, jnp.bfloat16)]
    if not last:
        out_shape.append(jax.ShapeDtypeStruct(past.shape, jnp.bfloat16))
        out_shape.append(jax.ShapeDtypeStruct(place.shape, place.dtype))
    return pl.pallas_call(
        functools.partial(layer_kernel, turn, last),
        out_shape=out_shape,
        in_specs=[whole] * len(operands),
        out_specs=[whole] * len(out_shape),
        scratch_shapes=[pltpu.VMEM((3, (2 + frames) * cols, 3 * chans), jnp.bfloat16)],
        compiler_params=pltpu.CompilerParams(vmem_limit_bytes=8 * mebi),
        cost_estimate=pl.CostEstimate(flops=1000, bytes_accessed=1000, transcendentals=0),
        name="layer",
    )(*operands)


def held(weight, place, past_shape):
    def kernel(source, place, target, first_place, past, sem):
        copy = pltpu.make_async_copy(source, target, sem)
        copy.start()
        first_place[...] = place[...]
        past[...] = jnp.zeros(past.shape, past.dtype)
        copy.wait()

    return pl.pallas_call(
        kernel,
        out_shape=[
            pltpu.VMEM(weight.shape, weight.dtype),
            jax.ShapeDtypeStruct(place.shape, place.dtype),
            jax.ShapeDtypeStruct(past_shape, jnp.bfloat16),
        ],
        in_specs=[pl.BlockSpec(memory_space=pltpu.HBM), whole],
        out_specs=[whole] * 3,
        scratch_shapes=[pltpu.SemaphoreType.DMA],
        compiler_params=pltpu.CompilerParams(vmem_limit_bytes=8 * mebi),
        cost_estimate=pl.CostEstimate(
            flops=0, bytes_accessed=2 * weight.size * 2, transcendentals=0
        ),
        name="held",
    )(pltpu.with_memory_space_constraint(weight, pltpu.HBM), place)


def body(latents, conv_weight, gain, bias):
    sections = lax.axis_size("section")
    row_count = lax.axis_size("rows")
    section_id = lax.axis_index("section")
    row_id = lax.axis_index("rows")
    cols, chans = latents.shape[3:]
    weight = conv_weight[0].reshape(9, 3 * chans, chans)
    local = latents[0, :, 0]
    items = sections
    steps = LAG * (sections - 1) + items

    def on_walk(r):
        line, at = divmod(r, CHIPS_X * CORES)
        chip, core = divmod(at, CORES)
        return (line * CHIPS_X + (CHIPS_X - 1 - chip if line % 2 else chip)) * CORES + core

    walk = {r: on_walk(r) for r in range(row_count)}
    same_row = {r: r for r in range(row_count)}
    partner = {r: r ^ 1 for r in range(row_count)}
    across = {walk[r]: walk[(r + 1 if r % 2 else r - 1) % row_count] for r in range(row_count)}
    same_section = {s: s for s in range(sections)}
    onward = {s: (s + 1) % sections for s in range(sections)}

    def move(x, next_section, next_row, but=()):
        pairs = [
            (s * row_count + r, s * row_count + r)
            if s in but
            else (s * row_count + r, next_section[s] * row_count + next_row[r])
            for s in range(sections)
            for r in range(row_count)
        ]
        return lax.ppermute(x, ("section", "rows"), pairs)

    def place_of(item, step):
        return (step - item) // LAG % sections

    def to(routes):
        route = dict(routes)
        free = [s for s in range(sections) if s not in route.values()]
        left = [s for s in range(sections) if s not in route]
        still = [s for s in left if s in free]
        free = [s for s in free if s not in still]
        left = [s for s in left if s not in still]
        route.update(zip(left, free))
        return lambda x: move(x, route, walk, still)

    def stream(step, items_there):
        return [i for i in items_there if (step - i) % LAG == 0]

    odd = row_id % 2
    edge = (row_id == walk[0]) | (row_id == walk[row_count - 1])
    lines = jnp.stack([-LAG * section_id, odd, edge.astype(jnp.int32)])
    place = jnp.broadcast_to(jnp.pad(lines, (0, 5))[:, None], (8, 128)).astype(jnp.int32)

    own = {step: to({step: 0})(local) for step in range(LAG)}
    handed = {
        step: to({i: place_of(i, step) for i in stream(step, range(LAG, items))})(local)
        for step in range(LAG)
    }
    leaving = {
        steps - 4: stream(steps - 4, range(items - 3)),
        steps - 3: stream(steps - 3, range(items - 2)),
        steps - 2: [items - 2],
        steps - 1: [items - 1],
    }
    weight, place, past = held(weight, place, (3, 2 * cols, 3 * chans))
    own[0], place = lax.optimization_barrier((own[0], place))
    home = {}
    decoded = None
    for step in range(steps):
        mine = own.pop(step)
        if step - LAG in home:
            mine, home[step - LAG] = lax.optimization_barrier((mine, home[step - LAG]))
        other = move(mine, same_section, partner)
        halo = move(mine, same_section, across)
        last = step == steps - 1
        sent, *carried = layer(
            last, place, mine, other, halo, past, weight, gain, bias, handed.get(step, mine)
        )
        if not last:
            past, place = carried
        if step + LAG < steps:
            own[step + LAG] = move(sent, onward, same_row)
        if step in leaving:
            home[step] = to({place_of(i, step): i for i in leaving[step]})(sent)
    for step, there in leaving.items():
        here = functools.reduce(jnp.logical_or, [section_id == i for i in there])
        decoded = home[step] if decoded is None else jnp.where(here, home[step], decoded)
    return decoded[None, :, None]


def solution(mesh):
    in_specs = (
        P("section", None, "rows", None, None),
        P("section", None, None, None, None, None),
        P("section", None),
        P("section", None),
    )
    out_specs = P("section", None, "rows", None, None)
    return jax.shard_map(body, mesh=mesh, in_specs=in_specs, out_specs=out_specs, check_vma=False)
```

```python
import functools
import itertools
import jax
import jax.numpy as jnp
from jax import lax
from jax.experimental import pallas as pl
from jax.experimental.pallas import tpu as pltpu
from jax.sharding import PartitionSpec as P

epsilon = 1e-06
LAG = 3
CORES = 2
CHIPS_X = 4
OWN, OTHER, HALO = range(3)
AGE, ODD, EDGE = range(3)
mebi = 1024 * 1024
whole = pl.BlockSpec(memory_space=pltpu.VMEM)


def activated(widened, gain_row):
    mean_square = jnp.mean(widened * widened, axis=-1, keepdims=True)
    normed = widened * lax.rsqrt(mean_square + epsilon) * gain_row
    return normed / (1.0 + jnp.exp(-normed))


def layer_kernel(turn, last, place, own, other, halo, past, weight, gain, bias, handed, *rest):
    sent, taps = rest[0], rest[-1]
    frames, cols, chans = own.shape
    rows = frames * cols
    kept = 2 * cols
    age = place[AGE : AGE + 1, :1]
    col = lax.broadcasted_iota(jnp.int32, (rows, chans), 0) % cols
    values = own[...].reshape(rows, chans).astype(jnp.float32)
    total = values + bias[...]
    odd = place[ODD, 0]
    for which, arrived in enumerate((own, other, halo)):
        if which != OWN:
            values = arrived[...].reshape(rows, chans).astype(jnp.float32)
        old = past[which].astype(jnp.float32)
        taps[which, :kept] = jnp.where(age == 0, 0.0, old).astype(jnp.bfloat16)
        act = activated(values, gain[...])
        if which == HALO:
            act = jnp.where(place[EDGE : EDGE + 1, :1] > 0, 0.0, act)
        left = jnp.where(col == 0, 0.0, pltpu.roll(act, 1, 0))
        right = jnp.where(col == cols - 1, 0.0, pltpu.roll(act, rows - 1, 0))
        taps[which, kept:, :chans] = left.astype(jnp.bfloat16)
        taps[which, kept:, chans : 2 * chans] = act.astype(jnp.bfloat16)
        taps[which, kept:, 2 * chans :] = right.astype(jnp.bfloat16)
        tap_r = (1, 2 - 2 * odd, 2 * odd)[which]
        for i in range(3):
            total += jnp.dot(
                taps[which, i * cols : i * cols + rows, :],
                weight[3 * i + tap_r],
                preferred_element_type=jnp.float32,
            )
    as_it_came = handed[...].reshape(rows, chans).astype(jnp.float32)
    waits = (age < turn // LAG - turn) | (age >= turn)
    total = jnp.where(waits, as_it_came, total)
    sent[...] = total.astype(jnp.bfloat16).reshape(frames, cols, chans)
    if not last:
        recent, next_place = rest[1:3]
        recent[...] = taps[:, rows:, :]
        line = lax.broadcasted_iota(jnp.int32, place.shape, 0)
        next_place[...] = place[...] + jnp.where(line == AGE, 1, 0)


def layer(last, place, own, other, halo, past, weight, gain, bias, handed):
    frames, cols, chans = own.shape
    turn = LAG * lax.axis_size("section")
    operands = [place, own, other, halo, past, weight, gain, bias, handed]
    out_shape = [jax.ShapeDtypeStruct(own.shape, jnp.bfloat16)]
    if not last:
        out_shape.append(jax.ShapeDtypeStruct(past.shape, jnp.bfloat16))
        out_shape.append(jax.ShapeDtypeStruct(place.shape, place.dtype))
    return pl.pallas_call(
        functools.partial(layer_kernel, turn, last),
        out_shape=out_shape,
        in_specs=[whole] * len(operands),
        out_specs=[whole] * len(out_shape),
        scratch_shapes=[pltpu.VMEM((3, (2 + frames) * cols, 3 * chans), jnp.bfloat16)],
        compiler_params=pltpu.CompilerParams(vmem_limit_bytes=8 * mebi),
        cost_estimate=pl.CostEstimate(flops=1000, bytes_accessed=1000, transcendentals=0),
        name="layer",
    )(*operands)


def held(weight, place, past_shape):
    def kernel(source, place, target, first_place, past, sem):
        copy = pltpu.make_async_copy(source, target, sem)
        copy.start()
        first_place[...] = place[...]
        past[...] = jnp.zeros(past.shape, past.dtype)
        copy.wait()

    return pl.pallas_call(
        kernel,
        out_shape=[
            pltpu.VMEM(weight.shape, weight.dtype),
            jax.ShapeDtypeStruct(place.shape, place.dtype),
            jax.ShapeDtypeStruct(past_shape, jnp.bfloat16),
        ],
        in_specs=[pl.BlockSpec(memory_space=pltpu.HBM), whole],
        out_specs=[whole] * 3,
        scratch_shapes=[pltpu.SemaphoreType.DMA],
        compiler_params=pltpu.CompilerParams(vmem_limit_bytes=8 * mebi),
        cost_estimate=pl.CostEstimate(
            flops=0, bytes_accessed=2 * weight.size * 2, transcendentals=0
        ),
        name="held",
    )(pltpu.with_memory_space_constraint(weight, pltpu.HBM), place)


def body(latents, conv_weight, gain, bias):
    sections = lax.axis_size("section")
    row_count = lax.axis_size("rows")
    section_id = lax.axis_index("section")
    row_id = lax.axis_index("rows")
    cols, chans = latents.shape[3:]
    weight = conv_weight[0].reshape(9, 3 * chans, chans)
    local = latents[0, :, 0]
    items = sections
    steps = LAG * (sections - 1) + items

    def on_walk(r):
        line, at = divmod(r, CHIPS_X * CORES)
        chip, core = divmod(at, CORES)
        return (line * CHIPS_X + (CHIPS_X - 1 - chip if line % 2 else chip)) * CORES + core

    walk = {r: on_walk(r) for r in range(row_count)}
    same_row = {r: r for r in range(row_count)}
    partner = {r: r ^ 1 for r in range(row_count)}
    across = {walk[r]: walk[(r + 1 if r % 2 else r - 1) % row_count] for r in range(row_count)}
    same_section = {s: s for s in range(sections)}
    onward = {s: (s + 1) % sections for s in range(sections)}

    def move(x, next_section, next_row, but=()):
        pairs = [
            (s * row_count + r, s * row_count + r)
            if s in but
            else (s * row_count + r, next_section[s] * row_count + next_row[r])
            for s in range(sections)
            for r in range(row_count)
        ]
        return lax.ppermute(x, ("section", "rows"), pairs)

    def place_of(item, step):
        return (step - item) // LAG % sections

    def hops(s, t):
        return min((s - t) % sections, (t - s) % sections)

    def to(routes):
        route = dict(routes)
        free = [s for s in range(sections) if s not in route.values()]
        left = [s for s in range(sections) if s not in route]
        still = [s for s in left if s in free]
        free = [s for s in free if s not in still]
        left = [s for s in left if s not in still]
        while left:
            s, t = min(itertools.product(left, free), key=lambda p: hops(*p))
            route[s] = t
            left.remove(s)
            free.remove(t)
        return lambda x: move(x, route, walk, still)

    def stream(step, items_there):
        return [i for i in items_there if (step - i) % LAG == 0]

    odd = row_id % 2
    edge = (row_id == walk[0]) | (row_id == walk[row_count - 1])
    lines = jnp.stack([-LAG * section_id, odd, edge.astype(jnp.int32)])
    place = jnp.broadcast_to(jnp.pad(lines, (0, 5))[:, None], (8, 128)).astype(jnp.int32)

    own = {step: to({step: 0})(local) for step in range(LAG)}
    handed = {
        step: to({i: place_of(i, step) for i in stream(step, range(LAG, items))})(local)
        for step in range(LAG)
    }
    leaving = {step: stream(step, range(items)) for step in range(steps - LAG, steps)}
    weight, place, past = held(weight, place, (3, 2 * cols, 3 * chans))
    own[0], place = lax.optimization_barrier((own[0], place))
    home = {}
    decoded = None
    for step in range(steps):
        mine = own.pop(step)
        other = move(mine, same_section, partner)
        halo = move(mine, same_section, across)
        last = step == steps - 1
        sent, *carried = layer(
            last, place, mine, other, halo, past, weight, gain, bias, handed.get(step, mine)
        )
        if not last:
            past, place = carried
        if step + LAG < steps:
            own[step + LAG] = move(sent, onward, same_row)
        if step in leaving:
            home[step] = to({place_of(i, step): i for i in leaving[step]})(sent)
    for step, there in leaving.items():
        here = functools.reduce(jnp.logical_or, [section_id == i for i in there])
        decoded = home[step] if decoded is None else jnp.where(here, home[step], decoded)
    return decoded[None, :, None]


def solution(mesh):
    in_specs = (
        P("section", None, "rows", None, None),
        P("section", None, None, None, None, None),
        P("section", None),
        P("section", None),
    )
    out_specs = P("section", None, "rows", None, None)
    return jax.shard_map(body, mesh=mesh, in_specs=in_specs, out_specs=out_specs, check_vma=False)
```

```python
import functools
import jax
import jax.numpy as jnp
from jax import lax
from jax.experimental import pallas as pl
from jax.experimental.pallas import tpu as pltpu
from jax.sharding import PartitionSpec as P

epsilon = 1e-06
LAG = 2
CORES = 2
CHIPS_X = 4
OWN, OTHER, HALO = range(3)
AGE, ODD, EDGE, SECTION = range(4)
mebi = 1024 * 1024
whole = pl.BlockSpec(memory_space=pltpu.VMEM)


def activated(widened, gain_row):
    mean_square = jnp.mean(widened * widened, axis=-1, keepdims=True)
    normed = widened * lax.rsqrt(mean_square + epsilon) * gain_row
    return normed / (1.0 + jnp.exp(-normed))


def layer_kernel(last, fed, place, own, other, halo, past, weight, gain, bias, *rest):
    taps = rest[-1]
    frames, cols, chans = own.shape
    rows = frames * cols
    kept = 2 * cols
    age = place[AGE : AGE + 1, :1]
    col = lax.broadcasted_iota(jnp.int32, (rows, chans), 0) % cols
    values = own[...].reshape(rows, chans).astype(jnp.float32)
    total = values + bias[...]
    odd = place[ODD, 0]
    for which, arrived in enumerate((own, other, halo)):
        if which != OWN:
            values = arrived[...].reshape(rows, chans).astype(jnp.float32)
        old = past[which].astype(jnp.float32)
        taps[which, :kept] = jnp.where(age == 0, 0.0, old).astype(jnp.bfloat16)
        act = activated(values, gain[...])
        if which == HALO:
            act = jnp.where(place[EDGE : EDGE + 1, :1] > 0, 0.0, act)
        left = jnp.where(col == 0, 0.0, pltpu.roll(act, 1, 0))
        right = jnp.where(col == cols - 1, 0.0, pltpu.roll(act, rows - 1, 0))
        taps[which, kept:, :chans] = left.astype(jnp.bfloat16)
        taps[which, kept:, chans : 2 * chans] = act.astype(jnp.bfloat16)
        taps[which, kept:, 2 * chans :] = right.astype(jnp.bfloat16)
        tap_r = (1, 2 - 2 * odd, 2 * odd)[which]
        for i in range(3):
            total += jnp.dot(
                taps[which, i * cols : i * cols + rows, :],
                weight[3 * i + tap_r],
                preferred_element_type=jnp.float32,
            )
    if fed:
        block = rest[0][...].reshape(rows, chans).astype(jnp.float32)
        feeds = age + place[SECTION : SECTION + 1, :1] == -LAG
        total = jnp.where(feeds, block, total)
        rest = rest[1:]
    sent, taps = rest[0], rest[-1]
    sent[...] = total.astype(jnp.bfloat16).reshape(frames, cols, chans)
    if not last:
        recent, next_place = rest[1:3]
        recent[...] = taps[:, rows:, :]
        line = lax.broadcasted_iota(jnp.int32, place.shape, 0)
        next_place[...] = place[...] + jnp.where(line == AGE, 1, 0)


def layer(last, place, own, other, halo, past, weight, gain, bias, block):
    frames, cols, chans = own.shape
    operands = [place, own, other, halo, past, weight, gain, bias]
    fed = block is not None
    if fed:
        operands.append(block)
    out_shape = [jax.ShapeDtypeStruct(own.shape, jnp.bfloat16)]
    if not last:
        out_shape.append(jax.ShapeDtypeStruct(past.shape, jnp.bfloat16))
        out_shape.append(jax.ShapeDtypeStruct(place.shape, place.dtype))
    return pl.pallas_call(
        functools.partial(layer_kernel, last, fed),
        out_shape=out_shape,
        in_specs=[whole] * len(operands),
        out_specs=[whole] * len(out_shape),
        scratch_shapes=[pltpu.VMEM((3, (2 + frames) * cols, 3 * chans), jnp.bfloat16)],
        compiler_params=pltpu.CompilerParams(vmem_limit_bytes=8 * mebi),
        cost_estimate=pl.CostEstimate(flops=1000, bytes_accessed=1000, transcendentals=0),
        name="layer",
    )(*operands)


def held(weight, place, past_shape):
    def kernel(source, place, target, first_place, past, sem):
        copy = pltpu.make_async_copy(source, target, sem)
        copy.start()
        first_place[...] = place[...]
        past[...] = jnp.zeros(past.shape, past.dtype)
        copy.wait()

    return pl.pallas_call(
        kernel,
        out_shape=[
            pltpu.VMEM(weight.shape, weight.dtype),
            jax.ShapeDtypeStruct(place.shape, place.dtype),
            jax.ShapeDtypeStruct(past_shape, jnp.bfloat16),
        ],
        in_specs=[pl.BlockSpec(memory_space=pltpu.HBM), whole],
        out_specs=[whole] * 3,
        scratch_shapes=[pltpu.SemaphoreType.DMA],
        compiler_params=pltpu.CompilerParams(vmem_limit_bytes=8 * mebi),
        cost_estimate=pl.CostEstimate(
            flops=0, bytes_accessed=2 * weight.size * 2, transcendentals=0
        ),
        name="held",
    )(pltpu.with_memory_space_constraint(weight, pltpu.HBM), place)


def body(latents, conv_weight, gain, bias):
    sections = lax.axis_size("section")
    row_count = lax.axis_size("rows")
    section_id = lax.axis_index("section")
    row_id = lax.axis_index("rows")
    cols, chans = latents.shape[3:]
    weight = conv_weight[0].reshape(9, 3 * chans, chans)
    local = latents[0, :, 0]
    items = sections
    steps = LAG * (sections - 1) + items

    def on_walk(r):
        line, at = divmod(r, CHIPS_X * CORES)
        chip, core = divmod(at, CORES)
        return (line * CHIPS_X + (CHIPS_X - 1 - chip if line % 2 else chip)) * CORES + core

    walk = {r: on_walk(r) for r in range(row_count)}
    same_row = {r: r for r in range(row_count)}
    partner = {r: r ^ 1 for r in range(row_count)}
    across = {walk[r]: walk[(r + 1 if r % 2 else r - 1) % row_count] for r in range(row_count)}
    same_section = {s: s for s in range(sections)}

    def move(x, next_section, next_row):
        pairs = [
            (s * row_count + r, next_section[s] * row_count + next_row[s][r])
            for s in range(sections)
            for r in range(row_count)
        ]
        return lax.ppermute(x, ("section", "rows"), pairs)

    def all_rows(rows):
        return dict.fromkeys(range(sections), rows)

    def hop(x, step):
        low, high, rows = 0, sections - 1, all_rows(same_row)
        if step + LAG < items:
            high = step + LAG
            rows[high] = walk
        elif step >= LAG * (sections - 1):
            low = step - LAG * (sections - 1)
            rows[sections - 1] = walk
        route = dict(same_section)
        route.update({s: s + 1 if s < high else low for s in range(low, high + 1)})
        return move(x, route, rows)

    odd = row_id % 2
    edge = (row_id == walk[0]) | (row_id == walk[row_count - 1])
    lines = jnp.stack([-LAG * section_id, odd, edge.astype(jnp.int32), section_id])
    place = jnp.broadcast_to(jnp.pad(lines, (0, 4))[:, None], (8, 128)).astype(jnp.int32)

    own = {0: move(local, same_section, all_rows(walk))}
    for item in range(1, LAG):
        swap = {**same_section, 0: item, item: 0}
        rows = {**all_rows(same_row), 0: walk, item: walk}
        own[item] = move(local, swap, rows)
    weight, place, past = held(weight, place, (3, 2 * cols, 3 * chans))
    own[0], place = lax.optimization_barrier((own[0], place))
    decoded = None
    for step in range(steps):
        mine = own.pop(step)
        other = move(mine, same_section, all_rows(partner))
        halo = move(mine, same_section, all_rows(across))
        last = step == steps - 1
        block = local if step + LAG < items else None
        sent, *carried = layer(
            last, place, mine, other, halo, past, weight, gain, bias, block
        )
        if last:
            arrived = move(sent, same_section, {**all_rows(same_row), sections - 1: walk})
        else:
            past, place = carried
            arrived = hop(sent, step)
            if step + LAG < steps:
                own[step + LAG] = arrived
        done = step - LAG * (sections - 1)
        if done >= 0:
            homes = section_id == done
            decoded = arrived if decoded is None else jnp.where(homes, arrived, decoded)
    return decoded[None, :, None]


def solution(mesh):
    in_specs = (
        P("section", None, "rows", None, None),
        P("section", None, None, None, None, None),
        P("section", None),
        P("section", None),
    )
    out_specs = P("section", None, "rows", None, None)
    return jax.shard_map(body, mesh=mesh, in_specs=in_specs, out_specs=out_specs, check_vma=False)
```

```python
import functools
import itertools
import jax
import jax.numpy as jnp
from jax import lax
from jax.experimental import pallas as pl
from jax.experimental.pallas import tpu as pltpu
from jax.sharding import PartitionSpec as P

epsilon = 1e-06
LAG = 2
CORES = 2
CHIPS_X = 4
OWN, OTHER, HALO = range(3)
AGE, ODD, EDGE = range(3)
mebi = 1024 * 1024
whole = pl.BlockSpec(memory_space=pltpu.VMEM)


def activated(widened, gain_row):
    mean_square = jnp.mean(widened * widened, axis=-1, keepdims=True)
    normed = widened * lax.rsqrt(mean_square + epsilon) * gain_row
    return normed / (1.0 + jnp.exp(-normed))


def row_kernel(which, turn, last, place, arrived, past, weight, gain, extra, *rest):
    taps = rest[-1]
    frames, cols, chans = arrived.shape
    rows = frames * cols
    kept = 2 * cols
    values = arrived[...].reshape(rows, chans).astype(jnp.float32)
    age = place[AGE : AGE + 1, :1]
    old = past[...].astype(jnp.float32)
    taps[:kept] = jnp.where(age == 0, 0.0, old).astype(jnp.bfloat16)
    act = activated(values, gain[...])
    if which == HALO:
        act = jnp.where(place[EDGE : EDGE + 1, :1] > 0, 0.0, act)
    col = lax.broadcasted_iota(jnp.int32, (rows, chans), 0) % cols
    left = jnp.where(col == 0, 0.0, pltpu.roll(act, 1, 0))
    right = jnp.where(col == cols - 1, 0.0, pltpu.roll(act, rows - 1, 0))
    taps[kept:, :chans] = left.astype(jnp.bfloat16)
    taps[kept:, chans : 2 * chans] = act.astype(jnp.bfloat16)
    taps[kept:, 2 * chans :] = right.astype(jnp.bfloat16)
    if which == OWN:
        total = values + extra[...]
        tap_r = 1
    else:
        total = extra[...]
        odd = place[ODD, 0]
        tap_r = 2 * odd if which == HALO else 2 - 2 * odd
    for i in range(3):
        total += jnp.dot(
            taps[i * cols : i * cols + rows, :],
            weight[3 * i + tap_r],
            preferred_element_type=jnp.float32,
        )
    if which == HALO:
        own, sent = rest[:2]
        as_it_came = own[...].reshape(rows, chans).astype(jnp.float32)
        waits = (age < turn // LAG - turn) | (age >= turn)
        total = jnp.where(waits, as_it_came, total)
        sent[...] = total.astype(jnp.bfloat16).reshape(frames, cols, chans)
    else:
        rest[0][...] = total
    if not last:
        recent = rest[2 if which == HALO else 1]
        recent[...] = taps[rows:, :]
        if which == HALO:
            line = lax.broadcasted_iota(jnp.int32, place.shape, 0)
            rest[3][...] = place[...] + jnp.where(line == AGE, 1, 0)


def row_taps(which, last, place, arrived, past, weight, gain, *extra):
    frames, cols, chans = arrived.shape
    rows = frames * cols
    operands = [place, arrived, past, weight, gain, *extra]
    turn = LAG * lax.axis_size("section")
    out_shape = [
        jax.ShapeDtypeStruct((rows, chans), jnp.float32),
        jax.ShapeDtypeStruct(past.shape, jnp.bfloat16),
    ]
    if which == HALO:
        out_shape[0] = jax.ShapeDtypeStruct(arrived.shape, jnp.bfloat16)
        out_shape.append(jax.ShapeDtypeStruct(place.shape, place.dtype))
    if last:
        out_shape = out_shape[:1]
    return pl.pallas_call(
        functools.partial(row_kernel, which, turn, last),
        out_shape=out_shape,
        in_specs=[whole] * len(operands),
        out_specs=[whole] * len(out_shape),
        scratch_shapes=[pltpu.VMEM(((2 + frames) * cols, 3 * chans), jnp.bfloat16)],
        compiler_params=pltpu.CompilerParams(vmem_limit_bytes=8 * mebi),
        cost_estimate=pl.CostEstimate(flops=1000, bytes_accessed=1000, transcendentals=0),
        name=("own_row", "other_row", "halo_row")[which],
    )(*operands)


def held(weight, place, past_shape):
    def kernel(source, place, target, first_place, *rest):
        *pasts, sem = rest
        copy = pltpu.make_async_copy(source, target, sem)
        copy.start()
        first_place[...] = place[...]
        for past in pasts:
            past[...] = jnp.zeros(past.shape, past.dtype)
        copy.wait()

    return pl.pallas_call(
        kernel,
        out_shape=[
            pltpu.VMEM(weight.shape, weight.dtype),
            jax.ShapeDtypeStruct(place.shape, place.dtype),
        ]
        + [jax.ShapeDtypeStruct(past_shape, jnp.bfloat16)] * 3,
        in_specs=[pl.BlockSpec(memory_space=pltpu.HBM), whole],
        out_specs=[whole] * 5,
        scratch_shapes=[pltpu.SemaphoreType.DMA],
        compiler_params=pltpu.CompilerParams(vmem_limit_bytes=8 * mebi),
        cost_estimate=pl.CostEstimate(
            flops=0, bytes_accessed=2 * weight.size * 2, transcendentals=0
        ),
        name="held",
    )(pltpu.with_memory_space_constraint(weight, pltpu.HBM), place)


def body(latents, conv_weight, gain, bias):
    sections = lax.axis_size("section")
    row_count = lax.axis_size("rows")
    section_id = lax.axis_index("section")
    row_id = lax.axis_index("rows")
    cols, chans = latents.shape[3:]
    weight = conv_weight[0].reshape(9, 3 * chans, chans)
    local = latents[0, :, 0]
    items = sections
    steps = LAG * (sections - 1) + items

    def on_walk(r):
        line, at = divmod(r, CHIPS_X * CORES)
        chip, core = divmod(at, CORES)
        return (line * CHIPS_X + (CHIPS_X - 1 - chip if line % 2 else chip)) * CORES + core

    walk = {r: on_walk(r) for r in range(row_count)}
    same_row = {r: r for r in range(row_count)}
    partner = {r: r ^ 1 for r in range(row_count)}
    across = {walk[r]: walk[(r + 1 if r % 2 else r - 1) % row_count] for r in range(row_count)}
    same_section = {s: s for s in range(sections)}
    onward = {s: (s + 1) % sections for s in range(sections)}

    def move(x, next_section, next_row, but=()):
        pairs = [
            (s * row_count + r, s * row_count + r)
            if s in but
            else (s * row_count + r, next_section[s] * row_count + next_row[r])
            for s in range(sections)
            for r in range(row_count)
        ]
        return lax.ppermute(x, ("section", "rows"), pairs)

    def place_of(item, step):
        return (step - item) // LAG % sections

    def hops(s, t):
        return min((s - t) % sections, (t - s) % sections)

    def to(routes):
        route = dict(routes)
        free = [s for s in range(sections) if s not in route.values()]
        left = [s for s in range(sections) if s not in route]
        still = [s for s in left if s in free]
        free = [s for s in free if s not in still]
        left = [s for s in left if s not in still]
        while left:
            s, t = min(itertools.product(left, free), key=lambda p: hops(*p))
            route[s] = t
            left.remove(s)
            free.remove(t)
        return lambda x: move(x, route, walk, still)

    def stream(step, items_there):
        return [i for i in items_there if (step - i) % LAG == 0]

    odd = row_id % 2
    edge = (row_id == walk[0]) | (row_id == walk[row_count - 1])
    lines = jnp.stack([-LAG * section_id, odd, edge.astype(jnp.int32)])
    place = jnp.broadcast_to(jnp.pad(lines, (0, 5))[:, None], (8, 128)).astype(jnp.int32)

    own = {step: to({step: 0})(local) for step in range(LAG)}
    handed = {
        step: to({i: place_of(i, step) for i in stream(step, range(LAG, items))})(local)
        for step in range(LAG)
    }
    weight, place, *pasts = held(weight, place, (2 * cols, 3 * chans))
    own[0], place = lax.optimization_barrier((own[0], place))
    decoded = None
    for step in range(steps):
        last = step == steps - 1
        mine = own.pop(step)
        other = move(mine, same_section, partner)
        halo = move(mine, same_section, across)
        total = bias
        for which, arrived in enumerate((mine, other, halo)):
            extra = [total, handed.get(step, mine)] if which == HALO else [total]
            total, *carried = row_taps(
                which, last, place, arrived, pasts[which], weight, gain, *extra
            )
            if not last:
                pasts[which] = carried[0]
        sent = total
        if not last:
            place = carried[1]
        if step + LAG < steps:
            own[step + LAG] = move(sent, onward, same_row)
        else:
            there = stream(step, range(items))
            home = to({place_of(i, step): i for i in there})(sent)
            here = functools.reduce(jnp.logical_or, [section_id == i for i in there])
            decoded = home if decoded is None else jnp.where(here, home, decoded)
    return decoded[None, :, None]


def solution(mesh):
    in_specs = (
        P("section", None, "rows", None, None),
        P("section", None, None, None, None, None),
        P("section", None),
        P("section", None),
    )
    out_specs = P("section", None, "rows", None, None)
    return jax.shard_map(body, mesh=mesh, in_specs=in_specs, out_specs=out_specs, check_vma=False)
```

```python
import functools
import itertools
import jax
import jax.numpy as jnp
from jax import lax
from jax.experimental import pallas as pl
from jax.experimental.pallas import tpu as pltpu
from jax.sharding import PartitionSpec as P

epsilon = 1e-06
LAG = 2
CORES = 2
CHIPS_X = 4
OWN, OTHER, HALO = range(3)
AGE, ODD, EDGE = range(3)
mebi = 1024 * 1024
whole = pl.BlockSpec(memory_space=pltpu.VMEM)


def activated(widened, gain_row):
    mean_square = jnp.mean(widened * widened, axis=-1, keepdims=True)
    normed = widened * lax.rsqrt(mean_square + epsilon) * gain_row
    return normed / (1.0 + jnp.exp(-normed))


def row_kernel(which, turn, last, place, arrived, past, weight, gain, extra, *rest):
    taps = rest[-1]
    frames, cols, chans = arrived.shape
    rows = frames * cols
    kept = 2 * cols
    values = arrived[...].reshape(rows, chans).astype(jnp.float32)
    age = place[AGE : AGE + 1, :1]
    old = past[...].astype(jnp.float32)
    taps[:kept] = jnp.where(age == 0, 0.0, old).astype(jnp.bfloat16)
    act = activated(values, gain[...])
    if which == HALO:
        act = jnp.where(place[EDGE : EDGE + 1, :1] > 0, 0.0, act)
    col = lax.broadcasted_iota(jnp.int32, (rows, chans), 0) % cols
    left = jnp.where(col == 0, 0.0, pltpu.roll(act, 1, 0))
    right = jnp.where(col == cols - 1, 0.0, pltpu.roll(act, rows - 1, 0))
    taps[kept:, :chans] = left.astype(jnp.bfloat16)
    taps[kept:, chans : 2 * chans] = act.astype(jnp.bfloat16)
    taps[kept:, 2 * chans :] = right.astype(jnp.bfloat16)
    if which == OWN:
        total = values + extra[...]
        tap_r = 1
    else:
        total = extra[...]
        odd = place[ODD, 0]
        tap_r = 2 * odd if which == HALO else 2 - 2 * odd
    for i in range(3):
        total += jnp.dot(
            taps[i * cols : i * cols + rows, :],
            weight[3 * i + tap_r],
            preferred_element_type=jnp.float32,
        )
    if which == HALO:
        own, sent = rest[:2]
        as_it_came = own[...].reshape(rows, chans).astype(jnp.float32)
        waits = (age < turn // LAG - turn) | (age >= turn)
        total = jnp.where(waits, as_it_came, total)
        sent[...] = total.astype(jnp.bfloat16).reshape(frames, cols, chans)
    else:
        rest[0][...] = total
    if not last:
        recent = rest[2 if which == HALO else 1]
        recent[...] = taps[rows:, :]
        if which == HALO:
            line = lax.broadcasted_iota(jnp.int32, place.shape, 0)
            rest[3][...] = place[...] + jnp.where(line == AGE, 1, 0)


def row_taps(which, last, place, arrived, past, weight, gain, *extra):
    frames, cols, chans = arrived.shape
    rows = frames * cols
    operands = [place, arrived, past, weight, gain, *extra]
    turn = LAG * lax.axis_size("section")
    out_shape = [
        jax.ShapeDtypeStruct((rows, chans), jnp.float32),
        jax.ShapeDtypeStruct(past.shape, jnp.bfloat16),
    ]
    if which == HALO:
        out_shape[0] = jax.ShapeDtypeStruct(arrived.shape, jnp.bfloat16)
        out_shape.append(jax.ShapeDtypeStruct(place.shape, place.dtype))
    if last:
        out_shape = out_shape[:1]
    return pl.pallas_call(
        functools.partial(row_kernel, which, turn, last),
        out_shape=out_shape,
        in_specs=[whole] * len(operands),
        out_specs=[whole] * len(out_shape),
        scratch_shapes=[pltpu.VMEM(((2 + frames) * cols, 3 * chans), jnp.bfloat16)],
        compiler_params=pltpu.CompilerParams(vmem_limit_bytes=8 * mebi),
        cost_estimate=pl.CostEstimate(flops=1000, bytes_accessed=1000, transcendentals=0),
        name=("own_row", "other_row", "halo_row")[which],
    )(*operands)


def held(weight, place, past_shape):
    def kernel(source, place, target, first_place, *rest):
        *pasts, sem = rest
        copy = pltpu.make_async_copy(source, target, sem)
        copy.start()
        first_place[...] = place[...]
        for past in pasts:
            past[...] = jnp.zeros(past.shape, past.dtype)
        copy.wait()

    return pl.pallas_call(
        kernel,
        out_shape=[
            pltpu.VMEM(weight.shape, weight.dtype),
            jax.ShapeDtypeStruct(place.shape, place.dtype),
        ]
        + [jax.ShapeDtypeStruct(past_shape, jnp.bfloat16)] * 3,
        in_specs=[pl.BlockSpec(memory_space=pltpu.HBM), whole],
        out_specs=[whole] * 5,
        scratch_shapes=[pltpu.SemaphoreType.DMA],
        compiler_params=pltpu.CompilerParams(vmem_limit_bytes=8 * mebi),
        cost_estimate=pl.CostEstimate(
            flops=0, bytes_accessed=2 * weight.size * 2, transcendentals=0
        ),
        name="held",
    )(pltpu.with_memory_space_constraint(weight, pltpu.HBM), place)


def body(latents, conv_weight, gain, bias):
    sections = lax.axis_size("section")
    row_count = lax.axis_size("rows")
    section_id = lax.axis_index("section")
    row_id = lax.axis_index("rows")
    cols, chans = latents.shape[3:]
    weight = conv_weight[0].reshape(9, 3 * chans, chans)
    local = latents[0, :, 0]
    items = sections
    steps = LAG * (sections - 1) + items

    def on_walk(r):
        line, at = divmod(r, CHIPS_X * CORES)
        chip, core = divmod(at, CORES)
        return (line * CHIPS_X + (CHIPS_X - 1 - chip if line % 2 else chip)) * CORES + core

    walk = {r: on_walk(r) for r in range(row_count)}
    same_row = {r: r for r in range(row_count)}
    partner = {r: r ^ 1 for r in range(row_count)}
    across = {walk[r]: walk[(r + 1 if r % 2 else r - 1) % row_count] for r in range(row_count)}
    same_section = {s: s for s in range(sections)}
    onward = {s: (s + 1) % sections for s in range(sections)}

    def move(x, next_section, next_row):
        pairs = [
            (s * row_count + r, next_section[s] * row_count + next_row[s][r])
            for s in range(sections)
            for r in range(row_count)
        ]
        return lax.ppermute(x, ("section", "rows"), pairs)

    def all_rows(rows):
        return dict.fromkeys(range(sections), rows)

    def place_of(item, step):
        return (step - item) // LAG % sections

    def hops(s, t):
        return min((s - t) % sections, (t - s) % sections)

    def to(routes, onward_from=()):
        route = {**routes, **{s: s + 1 for s in onward_from}}
        free = [s for s in range(sections) if s not in route.values()]
        left = [s for s in range(sections) if s not in route]
        while left:
            s, t = min(itertools.product(left, free), key=lambda p: hops(*p))
            route[s] = t
            left.remove(s)
            free.remove(t)
        rows = {**all_rows(same_row), **dict.fromkeys(routes, walk)}
        return lambda x: move(x, route, rows)

    def stream(step, items_there):
        return [i for i in items_there if (step - i) % LAG == 0]

    odd = row_id % 2
    edge = (row_id == walk[0]) | (row_id == walk[row_count - 1])
    lines = jnp.stack([-LAG * section_id, odd, edge.astype(jnp.int32)])
    place = jnp.broadcast_to(jnp.pad(lines, (0, 5))[:, None], (8, 128)).astype(jnp.int32)

    own = {step: to({step: 0})(local) for step in range(LAG)}
    handed = {
        step: to({i: place_of(i, step) for i in stream(step, range(LAG, items))})(local)
        for step in range(LAG)
    }
    weight, place, *pasts = held(weight, place, (2 * cols, 3 * chans))
    own[0], place = lax.optimization_barrier((own[0], place))
    decoded = None
    for step in range(steps):
        last = step == steps - 1
        mine = own.pop(step)
        other = move(mine, same_section, all_rows(partner))
        halo = move(mine, same_section, all_rows(across))
        total = bias
        for which, arrived in enumerate((mine, other, halo)):
            extra = [total, handed.get(step, mine)] if which == HALO else [total]
            total, *carried = row_taps(
                which, last, place, arrived, pasts[which], weight, gain, *extra
            )
            if not last:
                pasts[which] = carried[0]
        sent = total
        if not last:
            place = carried[1]
        through = range(0, items - LAG) if step + LAG < steps else range(items - LAG, items)
        there = stream(step, through) if step + 2 * LAG >= steps else []
        routes = {place_of(i, step): i for i in there}
        if step + LAG >= steps:
            arrived = to(routes)(sent)
        elif there:
            going_on = [place_of(i, step) for i in stream(step, range(items - LAG, items))]
            arrived = to(routes, going_on)(sent)
        else:
            arrived = move(sent, onward, all_rows(same_row))
        if step + LAG < steps:
            own[step + LAG] = arrived
        if there:
            here = functools.reduce(jnp.logical_or, [section_id == i for i in there])
            decoded = arrived if decoded is None else jnp.where(here, arrived, decoded)
    return decoded[None, :, None]


def solution(mesh):
    in_specs = (
        P("section", None, "rows", None, None),
        P("section", None, None, None, None, None),
        P("section", None),
        P("section", None),
    )
    out_specs = P("section", None, "rows", None, None)
    return jax.shard_map(body, mesh=mesh, in_specs=in_specs, out_specs=out_specs, check_vma=False)
```
